32 devices in a mesh: row: 8 (over z, x), col: 4 (over y, core).
Axes of the slice: x: 2, y: 2, z: 4, core: 2. Of those that a mesh axis runs over, the one named last changes fastest.
Arguments:
- amplitudes: float32 [3072, 4, 2048], P(('row', 'col')), may hold values from -6 to 6
- integrals: float32 [2048, 4, 2048], P('row', None, 'col'), may hold values from -0.0625 to 0.0625
Outputs:
- ladder: float32 [3072, 2048], P('col', 'row')
The draws below stay inside these ranges and needn't reach their ends.
All inputs are finite; a program needn't handle non-finite values.
Results may differ from the reference program's by a relative error of at most 0.0001.
Values sent between devices are 32-bit elements; how exact they have to be, the bound alone decides.
A program may use at most 64 MiB of HBM per device.

```python
import jax
import jax.numpy as jnp
from jax import lax

IJ = 3072
PANEL = 2048
PANELS = 4
AB = 2048


def steps_of(own_key, shape, shards, least, high):
    gain = 1.0
    for position, shards_of in shards:
        draws = jax.random.uniform(jax.random.fold_in(jax.random.fold_in(own_key, 6), position), (shards_of,), jnp.float32, least / len(shards), high / len(shards))
        gain = gain * jnp.repeat(jnp.exp(draws), shape[position] // shards_of).reshape((-1,) + (1,) * (len(shape) - 1 - position))
    return gain


def centred(own_key, extent, scale, most, cuts=(), held_as=jnp.bfloat16):
    drawn = jax.random.normal(own_key, extent, jnp.float32) * scale
    if len(cuts) > 0:
        drawn = steps_of(own_key, extent, cuts, -0.22, 0.18) * drawn
    return jnp.clip(drawn, min=-most, max=most).astype(held_as)


def setup_inputs(seed: int = 0) -> dict:
    streams_of = jax.random.split(jax.random.key(seed), 3)
    amplitudes = centred(streams_of[0], (IJ, PANELS, PANEL), 1.0, 6.0, ((0, 32),), jnp.float32)
    integrals = centred(streams_of[1], (AB, PANELS, PANEL), (PANEL * PANELS) ** -0.5, 0.0625, ((0, 8), (2, 4)), jnp.float32)
    return dict(amplitudes=amplitudes, integrals=integrals)


def reference(amplitudes, integrals):
    ladder = jnp.zeros((IJ, AB), jnp.float32)
    for panel in range(PANELS):
        panel_terms = jnp.dot(amplitudes[:, panel, :], integrals[:, panel, :].T, precision=lax.Precision.HIGHEST, preferred_element_type=jnp.float32)
        ladder = ladder + panel_terms
    return ladder
```

```python
import functools

import jax
import jax.numpy as jnp
from jax import lax
from jax.experimental import pallas as pl
from jax.experimental.pallas import tpu as pltpu
from jax.sharding import PartitionSpec as P

MESH = pl.DeviceIdType.MESH
WIDE = 256


def tile_of(extent, most):
    tile = most
    while extent % tile:
        tile //= 2
    return tile


def halves(x):
    high = x.astype(jnp.bfloat16)
    return high, (x - high.astype(jnp.float32)).astype(jnp.bfloat16)


def product(a, b):
    return lax.dot_general(a, b, (((1,), (1,)), ((), ())), preferred_element_type=jnp.float32)


def kernel(
    n_hi, n_lo, a_ref, v_ref, out_ref,
    a_all, v_all, a_high, a_low, v_high, v_low, partial, landed, final,
    own_sem, a_send, a_recv, v_send, v_recv, p_send, p_recv, f_sem,
):
    n_col = n_hi
    row = lax.axis_index("row")
    c = lax.axis_index("col")
    h = lax.div(row, n_lo)
    l = lax.rem(row, n_lo)
    w, panels, _ = a_ref.shape
    nb, _, kc = v_ref.shape
    rows = a_all.shape[0]
    kq = tile_of(kc, WIDE)
    n_chunk = kc // kq
    has = (h > 0, h < n_hi - 1)
    side_of = (-1, 1)

    barrier = pltpu.get_barrier_semaphore()

    def greet(device):
        pl.semaphore_signal(barrier, inc=1, device_id=device, device_id_type=MESH)

    offsets = [(dl, dc) for dl in range(n_lo) for dc in range(n_col) if (dl, dc) != (0, 0)]

    def peer(dl, dc):
        return h * n_lo + lax.rem(l + dl, n_lo), lax.rem(c + dc, n_col)

    for dl, dc in offsets:
        greet(peer(dl, dc))
    for side in range(2):
        @pl.when(has[side])
        def _():
            greet((row + side_of[side] * n_lo, c))

    @pl.when(c != h)
    def _():
        greet((c * n_lo + l, h))

    others = [jnp.where(condition, 1, 0) for condition in (*has, c != h)]
    pl.semaphore_wait(barrier, len(offsets) + sum(others))

    def v_copy(side, d, q):
        s = h - side_of[side] * d
        cols = pl.ds(q * kq, kq)
        source = v_ref.at[:, :, cols] if d == 0 else v_all.at[s, :, :, cols]
        return pltpu.make_async_remote_copy(
            src_ref=source,
            dst_ref=v_all.at[s, :, :, cols],
            send_sem=v_send.at[side, d, q],
            recv_sem=v_recv.at[side, d, q],
            device_id=(row + side_of[side] * n_lo, c),
            device_id_type=MESH,
        )

    def sends(side, d):
        s = h - side_of[side] * d
        return has[side] & (s >= 0) & (s < n_hi)

    def hears(side, d):
        s = h - side_of[side] * d
        return (s >= 0) & (s < n_hi)

    for q in range(n_chunk):
        for side in range(2):
            @pl.when(sends(side, 0))
            def _():
                v_copy(side, 0, q).start()

    def a_copy(dl, dc):
        to_row, to_col = peer(dl, dc)
        return pltpu.make_async_remote_copy(
            src_ref=a_ref.at[:, :, pl.ds(pl.multiple_of(to_col * kc, kc), kc)],
            dst_ref=a_all.at[pl.ds((l * n_col + c) * w, w)],
            send_sem=a_send.at[dl, dc],
            recv_sem=a_recv.at[dl, dc],
            device_id=(to_row, to_col),
            device_id_type=MESH,
        )

    for dl, dc in offsets:
        a_copy(dl, dc).start()
    own_v = pltpu.make_async_copy(v_ref, v_all.at[h], own_sem.at[0])
    own_v.start()
    own_a = pltpu.make_async_copy(
        a_ref.at[:, :, pl.ds(pl.multiple_of(c * kc, kc), kc)], a_all.at[pl.ds((l * n_col + c) * w, w)], own_sem.at[1]
    )
    own_a.start()

    def forward(d, q):
        for side in range(2):
            @pl.when(hears(side, d))
            def _():
                s = h - side_of[side] * d
                cols = pl.ds(q * kq, kq)
                pltpu.make_async_remote_copy(
                    src_ref=v_all.at[s, :, :, cols],
                    dst_ref=v_all.at[s, :, :, cols],
                    send_sem=v_send.at[side, d - 1, q],
                    recv_sem=v_recv.at[side, d - 1, q],
                    device_id=(row, c),
                    device_id_type=MESH,
                ).wait_recv()
                if d < n_hi - 1:
                    @pl.when(has[side])
                    def _():
                        v_copy(side, d, q).start()

    def take_a():
        own_a.wait()
        for dl, dc in offsets:
            from_l, from_c = lax.rem(l + n_lo - dl, n_lo), lax.rem(c + n_col - dc, n_col)
            pltpu.make_async_remote_copy(
                src_ref=a_all.at[pl.ds((from_l * n_col + from_c) * w, w)],
                dst_ref=a_all.at[pl.ds((from_l * n_col + from_c) * w, w)],
                send_sem=a_send.at[dl, dc],
                recv_sem=a_recv.at[dl, dc],
                device_id=(row, c),
                device_id_type=MESH,
            ).wait_recv()
        t = tile_of(rows, 32)

        @pl.loop(0, rows // t)
        def _(i):
            at = pl.ds(pl.multiple_of(i * t, t), t)
            for p in range(panels):
                a_high[at, pl.ds(p * kc, kc)], a_low[at, pl.ds(p * kc, kc)] = halves(a_all[at, p, :])

    def multiply(s, q):
        t = tile_of(nb, 32)

        @pl.loop(0, nb // t)
        def _(i):
            at = pl.ds(pl.multiple_of(i * t, t), t)
            for p in range(panels):
                v_high[at, pl.ds(p * kq, kq)], v_low[at, pl.ds(p * kq, kq)] = halves(
                    v_all[s, at, p, pl.ds(q * kq, kq)]
                )

        m = tile_of(rows, 256)

        @pl.loop(0, rows // m)
        def _(i):
            at = pl.ds(pl.multiple_of(i * m, m), m)
            total = None if q == 0 else partial[s, at, :]
            for p in range(panels):
                a_cols, v_cols = pl.ds(p * kc + q * kq, kq), pl.ds(p * kq, kq)
                ah, al = a_high[at, a_cols], a_low[at, a_cols]
                vh, vl = v_high[:, v_cols], v_low[:, v_cols]
                term = product(ah, vh) + (product(ah, vl) + product(al, vh))
                total = term if total is None else total + term
            partial[s, at, :] = total

    def p_copy(s, k):
        return pltpu.make_async_remote_copy(
            src_ref=partial.at[s],
            dst_ref=landed.at[c],
            send_sem=p_send.at[k],
            recv_sem=p_recv.at[c],
            device_id=(row, s),
            device_id_type=MESH,
        )

    def blocks(d):
        if d == 0:
            return [(0, None, h)]
        return [(2 * d - 1 + side, hears(side, d), h - side_of[side] * d) for side in range(2)]

    def compute(d, q):
        for k, condition, s in blocks(d):
            def run():
                multiply(s, q)
                if q == n_chunk - 1:
                    @pl.when(s != c)
                    def _():
                        p_copy(s, k).start()
            run() if condition is None else pl.when(condition)(run)

    chunks = range(n_chunk)
    for q in chunks:
        forward(1, q)
    take_a()
    own_v.wait()
    for q in chunks:
        compute(0, q)
    if n_hi > 2:
        forward(2, 0)
    for q in chunks:
        compute(1, q)
    for d in range(2, n_hi):
        for q in chunks:
            if (d, q) != (2, 0):
                forward(d, q)
            compute(d, q)

    for dc in range(1, n_col):
        from_c = lax.rem(c + dc, n_col)
        pltpu.make_async_remote_copy(
            src_ref=landed.at[from_c],
            dst_ref=landed.at[from_c],
            send_sem=p_send.at[0],
            recv_sem=p_recv.at[from_c],
            device_id=(row, c),
            device_id_type=MESH,
        ).wait_recv()
    t = tile_of(rows, 64)

    @pl.loop(0, rows // t)
    def _(i):
        at = pl.ds(pl.multiple_of(i * t, t), t)
        total = partial[c, at, :]
        for dc in range(1, n_col):
            total = total + landed[lax.rem(c + dc, n_col), at, :]
        final[at, :] = total

    @pl.when(c != h)
    def _():
        copy = pltpu.make_async_remote_copy(
            src_ref=final,
            dst_ref=out_ref,
            send_sem=f_sem.at[0],
            recv_sem=f_sem.at[1],
            device_id=(c * n_lo + l, h),
            device_id_type=MESH,
        )
        copy.start()
        copy.wait()

    @pl.when(c == h)
    def _():
        copy = pltpu.make_async_copy(final, out_ref, f_sem.at[0])
        copy.start()
        copy.wait()

    for dl, dc in offsets:
        a_copy(dl, dc).wait_send()
    for side in range(2):
        for d in range(n_hi - 1):
            @pl.when(sends(side, d))
            def _():
                for q in chunks:
                    v_copy(side, d, q).wait_send()
    for d in range(n_hi):
        for k, condition, s in blocks(d):
            there = s != c if condition is None else condition & (s != c)

            @pl.when(there)
            def _():
                p_copy(s, k).wait_send()


def per_device(amplitudes, integrals):
    n_row = lax.axis_size("row")
    n_col = lax.axis_size("col")
    n_lo = n_row // n_col
    w, panels, _ = amplitudes.shape
    nb, _, kc = integrals.shape
    rows = w * n_lo * n_col
    kq = tile_of(kc, WIDE)
    n_chunk = kc // kq
    f32, bf16 = jnp.float32, jnp.bfloat16
    dma = pltpu.SemaphoreType.DMA
    return pl.pallas_call(
        functools.partial(kernel, n_col, n_lo),
        out_shape=jax.ShapeDtypeStruct((rows, nb), f32),
        in_specs=[pl.BlockSpec(memory_space=pl.ANY)] * 2,
        out_specs=pl.BlockSpec(memory_space=pl.ANY),
        scratch_shapes=[
            pltpu.VMEM((rows, panels, kc), f32),
            pltpu.VMEM((n_col, nb, panels, kc), f32),
            pltpu.VMEM((rows, panels * kc), bf16),
            pltpu.VMEM((rows, panels * kc), bf16),
            pltpu.VMEM((nb, panels * kq), bf16),
            pltpu.VMEM((nb, panels * kq), bf16),
            pltpu.VMEM((n_col, rows, nb), f32),
            pltpu.VMEM((n_col, rows, nb), f32),
            pltpu.VMEM((rows, nb), f32),
            dma((2,)),
            dma((n_lo, n_col)),
            dma((n_lo, n_col)),
            dma((2, n_col, n_chunk)),
            dma((2, n_col, n_chunk)),
            dma((2 * n_col,)),
            dma((n_col,)),
            dma((2,)),
        ],
        compiler_params=pltpu.CompilerParams(
            collective_id=0, has_side_effects=True, vmem_limit_bytes=48 * 2**20
        ),
        cost_estimate=pl.CostEstimate(
            flops=6 * rows * nb * n_col * panels * kc, bytes_accessed=4 * (amplitudes.size + integrals.size), transcendentals=0
        ),
    )(amplitudes, integrals)


def solution(mesh):
    in_specs = (P(("row", "col"), None, None), P("row", None, "col"))
    out_specs = P("col", "row")
    return jax.shard_map(
        per_device, mesh=mesh, in_specs=in_specs, out_specs=out_specs, check_vma=False
    )
```

```python
import functools

import jax
import jax.numpy as jnp
from jax import lax
from jax.experimental import pallas as pl
from jax.experimental.pallas import tpu as pltpu
from jax.sharding import PartitionSpec as P

MESH = pl.DeviceIdType.MESH
WIDE = 256


def tile_of(extent, most):
    tile = most
    while extent % tile:
        tile //= 2
    return tile


def halves(x):
    high = x.astype(jnp.bfloat16)
    return high, (x - high.astype(jnp.float32)).astype(jnp.bfloat16)


def product(a, b):
    return lax.dot_general(a, b, (((1,), (1,)), ((), ())), preferred_element_type=jnp.float32)


def kernel(
    n_hi, n_lo, a_ref, v_ref, out_ref,
    a_all, v_all, a_high, a_low, v_high, v_low, partial, landed, final,
    own_sem, a_send, a_recv, v_send, v_recv, p_send, p_recv, f_sem,
):
    n_col = n_hi
    row = lax.axis_index("row")
    c = lax.axis_index("col")
    h = lax.div(row, n_lo)
    l = lax.rem(row, n_lo)
    w, panels, _ = a_ref.shape
    nb, _, kc = v_ref.shape
    rows = a_all.shape[0]
    kq = tile_of(kc, WIDE)
    n_chunk = kc // kq
    has = (h > 0, h < n_hi - 1)
    side_of = (-1, 1)

    barrier = pltpu.get_barrier_semaphore()

    def greet(device):
        pl.semaphore_signal(barrier, inc=1, device_id=device, device_id_type=MESH)

    offsets = [(dl, dc) for dl in range(n_lo) for dc in range(n_col) if (dl, dc) != (0, 0)]

    def peer(dl, dc):
        return h * n_lo + lax.rem(l + dl, n_lo), lax.rem(c + dc, n_col)

    for dl, dc in offsets:
        greet(peer(dl, dc))
    for side in range(2):
        @pl.when(has[side])
        def _():
            greet((row + side_of[side] * n_lo, c))

    @pl.when(c != h)
    def _():
        greet((c * n_lo + l, h))

    others = [jnp.where(condition, 1, 0) for condition in (*has, c != h)]
    pl.semaphore_wait(barrier, len(offsets) + sum(others))

    def v_copy(side, d, q):
        s = h - side_of[side] * d
        cols = pl.ds(q * kq, kq)
        source = v_ref.at[:, :, cols] if d == 0 else v_all.at[s, :, :, cols]
        return pltpu.make_async_remote_copy(
            src_ref=source,
            dst_ref=v_all.at[s, :, :, cols],
            send_sem=v_send.at[side, d, q],
            recv_sem=v_recv.at[side, d, q],
            device_id=(row + side_of[side] * n_lo, c),
            device_id_type=MESH,
        )

    def sends(side, d):
        s = h - side_of[side] * d
        return has[side] & (s >= 0) & (s < n_hi)

    def hears(side, d):
        s = h - side_of[side] * d
        return (s >= 0) & (s < n_hi)

    for q in range(n_chunk):
        for side in range(2):
            @pl.when(sends(side, 0))
            def _():
                v_copy(side, 0, q).start()

    def a_copy(dl, dc):
        to_row, to_col = peer(dl, dc)
        return pltpu.make_async_remote_copy(
            src_ref=a_ref.at[:, :, pl.ds(pl.multiple_of(to_col * kc, kc), kc)],
            dst_ref=a_all.at[pl.ds((l * n_col + c) * w, w)],
            send_sem=a_send.at[dl, dc],
            recv_sem=a_recv.at[dl, dc],
            device_id=(to_row, to_col),
            device_id_type=MESH,
        )

    for dl, dc in offsets:
        a_copy(dl, dc).start()
    own_v = pltpu.make_async_copy(v_ref, v_all.at[h], own_sem.at[0])
    own_v.start()
    own_a = pltpu.make_async_copy(
        a_ref.at[:, :, pl.ds(pl.multiple_of(c * kc, kc), kc)], a_all.at[pl.ds((l * n_col + c) * w, w)], own_sem.at[1]
    )
    own_a.start()

    def forward(d, q):
        for side in range(2):
            @pl.when(hears(side, d))
            def _():
                s = h - side_of[side] * d
                cols = pl.ds(q * kq, kq)
                pltpu.make_async_remote_copy(
                    src_ref=v_all.at[s, :, :, cols],
                    dst_ref=v_all.at[s, :, :, cols],
                    send_sem=v_send.at[side, d - 1, q],
                    recv_sem=v_recv.at[side, d - 1, q],
                    device_id=(row, c),
                    device_id_type=MESH,
                ).wait_recv()
                if d < n_hi - 1:
                    @pl.when(has[side])
                    def _():
                        v_copy(side, d, q).start()

    def take_a():
        own_a.wait()
        for dl, dc in offsets:
            from_l, from_c = lax.rem(l + n_lo - dl, n_lo), lax.rem(c + n_col - dc, n_col)
            pltpu.make_async_remote_copy(
                src_ref=a_all.at[pl.ds((from_l * n_col + from_c) * w, w)],
                dst_ref=a_all.at[pl.ds((from_l * n_col + from_c) * w, w)],
                send_sem=a_send.at[dl, dc],
                recv_sem=a_recv.at[dl, dc],
                device_id=(row, c),
                device_id_type=MESH,
            ).wait_recv()
        t = tile_of(rows, 32)

        @pl.loop(0, rows // t)
        def _(i):
            at = pl.ds(pl.multiple_of(i * t, t), t)
            for p in range(panels):
                a_high[at, pl.ds(p * kc, kc)], a_low[at, pl.ds(p * kc, kc)] = halves(a_all[at, p, :])

    def multiply(s, q):
        t = tile_of(nb, 32)

        @pl.loop(0, nb // t)
        def _(i):
            at = pl.ds(pl.multiple_of(i * t, t), t)
            for p in range(panels):
                v_high[at, pl.ds(p * kq, kq)], v_low[at, pl.ds(p * kq, kq)] = halves(
                    v_all[s, at, p, pl.ds(q * kq, kq)]
                )

        m = tile_of(rows, 256)

        @pl.loop(0, rows // m)
        def _(i):
            at = pl.ds(pl.multiple_of(i * m, m), m)
            total = None if q == 0 else partial[s, at, :]
            for p in range(panels):
                a_cols, v_cols = pl.ds(p * kc + q * kq, kq), pl.ds(p * kq, kq)
                ah, al = a_high[at, a_cols], a_low[at, a_cols]
                vh, vl = v_high[:, v_cols], v_low[:, v_cols]
                term = product(ah, vh) + (product(ah, vl) + product(al, vh))
                total = term if total is None else total + term
            partial[s, at, :] = total

    def p_copy(s, k):
        return pltpu.make_async_remote_copy(
            src_ref=partial.at[s],
            dst_ref=landed.at[c],
            send_sem=p_send.at[k],
            recv_sem=p_recv.at[c],
            device_id=(row, s),
            device_id_type=MESH,
        )

    def blocks(d):
        if d == 0:
            return [(0, None, h)]
        return [(2 * d - 1 + side, hears(side, d), h - side_of[side] * d) for side in range(2)]

    def compute(d, q):
        for k, condition, s in blocks(d):
            def run():
                multiply(s, q)
                if q == n_chunk - 1:
                    @pl.when(s != c)
                    def _():
                        p_copy(s, k).start()
            run() if condition is None else pl.when(condition)(run)

    chunks = range(n_chunk)
    for q in chunks:
        forward(1, q)
    if n_hi > 2:
        forward(2, 0)
    take_a()
    own_v.wait()
    for q in chunks:
        compute(0, q)
    if n_hi > 2:
        for q in chunks[1:]:
            forward(2, q)
    for d in range(1, n_hi):
        for q in chunks:
            if d > 2:
                forward(d, q)
            compute(d, q)

    for dc in range(1, n_col):
        from_c = lax.rem(c + dc, n_col)
        pltpu.make_async_remote_copy(
            src_ref=landed.at[from_c],
            dst_ref=landed.at[from_c],
            send_sem=p_send.at[0],
            recv_sem=p_recv.at[from_c],
            device_id=(row, c),
            device_id_type=MESH,
        ).wait_recv()
    n_piece = f_sem.shape[1]
    step = rows // n_piece
    t = tile_of(step, 64)

    def far(k):
        part = pl.ds(k * step, step)
        return pltpu.make_async_remote_copy(
            src_ref=final.at[part],
            dst_ref=out_ref.at[part],
            send_sem=f_sem.at[0, k],
            recv_sem=f_sem.at[1, k],
            device_id=(c * n_lo + l, h),
            device_id_type=MESH,
        )

    def near(k):
        part = pl.ds(k * step, step)
        return pltpu.make_async_copy(final.at[part], out_ref.at[part], f_sem.at[0, k])

    for k in range(n_piece):
        @pl.loop(0, step // t)
        def _(i):
            at = pl.ds(pl.multiple_of(k * step + i * t, t), t)
            total = partial[c, at, :]
            for dc in range(1, n_col):
                total = total + landed[lax.rem(c + dc, n_col), at, :]
            final[at, :] = total

        for there, copy in ((c != h, far), (c == h, near)):
            @pl.when(there)
            def _():
                copy(k).start()

    for there, copy in ((c != h, far), (c == h, near)):
        @pl.when(there)
        def _():
            for k in range(n_piece):
                copy(k).wait()

    for dl, dc in offsets:
        a_copy(dl, dc).wait_send()
    for side in range(2):
        for d in range(n_hi - 1):
            @pl.when(sends(side, d))
            def _():
                for q in chunks:
                    v_copy(side, d, q).wait_send()
    for d in range(n_hi):
        for k, condition, s in blocks(d):
            there = s != c if condition is None else condition & (s != c)

            @pl.when(there)
            def _():
                p_copy(s, k).wait_send()


def per_device(amplitudes, integrals):
    n_row = lax.axis_size("row")
    n_col = lax.axis_size("col")
    n_lo = n_row // n_col
    w, panels, _ = amplitudes.shape
    nb, _, kc = integrals.shape
    rows = w * n_lo * n_col
    kq = tile_of(kc, WIDE)
    n_chunk = kc // kq
    f32, bf16 = jnp.float32, jnp.bfloat16
    dma = pltpu.SemaphoreType.DMA
    return pl.pallas_call(
        functools.partial(kernel, n_col, n_lo),
        out_shape=jax.ShapeDtypeStruct((rows, nb), f32),
        in_specs=[pl.BlockSpec(memory_space=pl.ANY)] * 2,
        out_specs=pl.BlockSpec(memory_space=pl.ANY),
        scratch_shapes=[
            pltpu.VMEM((rows, panels, kc), f32),
            pltpu.VMEM((n_col, nb, panels, kc), f32),
            pltpu.VMEM((rows, panels * kc), bf16),
            pltpu.VMEM((rows, panels * kc), bf16),
            pltpu.VMEM((nb, panels * kq), bf16),
            pltpu.VMEM((nb, panels * kq), bf16),
            pltpu.VMEM((n_col, rows, nb), f32),
            pltpu.VMEM((n_col, rows, nb), f32),
            pltpu.VMEM((rows, nb), f32),
            dma((2,)),
            dma((n_lo, n_col)),
            dma((n_lo, n_col)),
            dma((2, n_col, n_chunk)),
            dma((2, n_col, n_chunk)),
            dma((2 * n_col,)),
            dma((n_col,)),
            dma((2, tile_of(rows // 8, 4))),
        ],
        compiler_params=pltpu.CompilerParams(
            collective_id=0, has_side_effects=True, vmem_limit_bytes=48 * 2**20
        ),
        cost_estimate=pl.CostEstimate(
            flops=6 * rows * nb * n_col * panels * kc, bytes_accessed=4 * (amplitudes.size + integrals.size), transcendentals=0
        ),
    )(amplitudes, integrals)


def solution(mesh):
    in_specs = (P(("row", "col"), None, None), P("row", None, "col"))
    out_specs = P("col", "row")
    return jax.shard_map(
        per_device, mesh=mesh, in_specs=in_specs, out_specs=out_specs, check_vma=False
    )
```

```python
import functools

import jax
import jax.numpy as jnp
from jax import lax
from jax.experimental import pallas as pl
from jax.experimental.pallas import tpu as pltpu
from jax.sharding import PartitionSpec as P

MESH = pl.DeviceIdType.MESH
WIDE = 256


def tile_of(extent, most):
    tile = most
    while extent % tile:
        tile //= 2
    return tile


def halves(x):
    high = x.astype(jnp.bfloat16)
    return high, (x - high.astype(jnp.float32)).astype(jnp.bfloat16)


def rows_at_once(extent, most):
    tile = tile_of(extent, most)
    return extent if tile % 16 else tile


def product(a, b):
    return lax.dot_general(a, b, (((1,), (1,)), ((), ())), preferred_element_type=jnp.float32)


def kernel(
    n_hi, n_lo, a_ref, v_ref, out_ref,
    a_all, v_all, a_high, a_low, v_high, v_low, partial, landed, final,
    own_sem, a_send, a_recv, v_send, v_recv, p_send, p_recv, f_send, f_recv,
):
    n_col = n_hi
    row = lax.axis_index("row")
    c = lax.axis_index("col")
    h = lax.div(row, n_lo)
    l = lax.rem(row, n_lo)
    w, panels, _ = a_ref.shape
    nb, _, kc = v_ref.shape
    step = partial.shape[2]
    kq = tile_of(kc, WIDE)
    n_chunk = kc // kq
    has = (h > 0, h < n_hi - 1)
    side_of = (-1, 1)

    barrier = pltpu.get_barrier_semaphore()

    def greet(device):
        pl.semaphore_signal(barrier, inc=1, device_id=device, device_id_type=MESH)

    offsets = [(dl, dc) for dl in range(n_lo) for dc in range(n_col) if (dl, dc) != (0, 0)]

    def peer(dl, dc):
        return h * n_lo + lax.rem(l + dl, n_lo), lax.rem(c + dc, n_col)

    for dl, dc in offsets:
        greet(peer(dl, dc))
    for side in range(2):
        @pl.when(has[side])
        def _():
            greet((row + side_of[side] * n_lo, c))

    def is_self(to_h, to_c):
        return (to_h == h) & (to_c == c)

    for j in range(n_col):
        @pl.when(jnp.logical_not(is_self(c, j)))
        def _():
            greet((c * n_lo + l, j))
    others = [jnp.where(condition, 1, 0) for condition in (*has, c != h)]
    pl.semaphore_wait(barrier, len(offsets) + n_hi - 1 + sum(others))

    def v_copy(side, d, q):
        s = h - side_of[side] * d
        cols = pl.ds(q * kq, kq)
        source = v_ref.at[:, :, cols] if d == 0 else v_all.at[s, :, :, cols]
        return pltpu.make_async_remote_copy(
            src_ref=source,
            dst_ref=v_all.at[s, :, :, cols],
            send_sem=v_send.at[side, d, q],
            recv_sem=v_recv.at[side, d, q],
            device_id=(row + side_of[side] * n_lo, c),
            device_id_type=MESH,
        )

    def sends(side, d):
        s = h - side_of[side] * d
        return has[side] & (s >= 0) & (s < n_hi)

    def hears(side, d):
        s = h - side_of[side] * d
        return (s >= 0) & (s < n_hi)

    for q in range(n_chunk):
        for side in range(2):
            @pl.when(sends(side, 0))
            def _():
                v_copy(side, 0, q).start()

    def a_copy(dl, dc):
        to_row, to_col = peer(dl, dc)
        return pltpu.make_async_remote_copy(
            src_ref=a_ref.at[:, :, pl.ds(pl.multiple_of(to_col * kc, kc), kc)],
            dst_ref=a_all.at[pl.ds((l * n_col + c) * w, w)],
            send_sem=a_send.at[dl, dc],
            recv_sem=a_recv.at[dl, dc],
            device_id=(to_row, to_col),
            device_id_type=MESH,
        )

    for dl, dc in offsets:
        a_copy(dl, dc).start()
    own_v = pltpu.make_async_copy(v_ref, v_all.at[h], own_sem.at[0])
    own_v.start()
    own_a = pltpu.make_async_copy(
        a_ref.at[:, :, pl.ds(pl.multiple_of(c * kc, kc), kc)], a_all.at[pl.ds((l * n_col + c) * w, w)], own_sem.at[1]
    )
    own_a.start()

    def forward(d, q):
        for side in range(2):
            @pl.when(hears(side, d))
            def _():
                s = h - side_of[side] * d
                cols = pl.ds(q * kq, kq)
                pltpu.make_async_remote_copy(
                    src_ref=v_all.at[s, :, :, cols],
                    dst_ref=v_all.at[s, :, :, cols],
                    send_sem=v_send.at[side, d - 1, q],
                    recv_sem=v_recv.at[side, d - 1, q],
                    device_id=(row, c),
                    device_id_type=MESH,
                ).wait_recv()
                if d < n_hi - 1:
                    @pl.when(has[side])
                    def _():
                        v_copy(side, d, q).start()

    def take_a():
        own_a.wait()
        for dl, dc in offsets:
            from_l, from_c = lax.rem(l + n_lo - dl, n_lo), lax.rem(c + n_col - dc, n_col)
            pltpu.make_async_remote_copy(
                src_ref=a_all.at[pl.ds((from_l * n_col + from_c) * w, w)],
                dst_ref=a_all.at[pl.ds((from_l * n_col + from_c) * w, w)],
                send_sem=a_send.at[dl, dc],
                recv_sem=a_recv.at[dl, dc],
                device_id=(row, c),
                device_id_type=MESH,
            ).wait_recv()
        t = rows_at_once(step, 32)

        @pl.loop(0, n_col)
        def _(i):
            @pl.loop(0, step // t)
            def _(j):
                at = pl.ds(0, t) if t == step else pl.ds(pl.multiple_of(j * t, t), t)
                for p in range(panels):
                    cols = pl.ds(p * kc, kc)
                    a_high[i, at, cols], a_low[i, at, cols] = halves(a_all[pl.ds(i * step + j * t, t), p, :])

    def multiply(s, q):
        t = tile_of(nb, 32)

        @pl.loop(0, nb // t)
        def _(i):
            at = pl.ds(pl.multiple_of(i * t, t), t)
            for p in range(panels):
                v_high[at, pl.ds(p * kq, kq)], v_low[at, pl.ds(p * kq, kq)] = halves(
                    v_all[s, at, p, pl.ds(q * kq, kq)]
                )

        @pl.loop(0, n_col)
        def _(i):
            total = None if q == 0 else partial[s, i]
            for p in range(panels):
                a_cols, v_cols = pl.ds(p * kc + q * kq, kq), pl.ds(p * kq, kq)
                ah, al = a_high[i, :, a_cols], a_low[i, :, a_cols]
                vh, vl = v_high[:, v_cols], v_low[:, v_cols]
                term = product(ah, vh) + (product(ah, vl) + product(al, vh))
                total = term if total is None else total + term
            partial[s, i] = total

    def p_copy(s, k, dc):
        to_c = lax.rem(c + dc, n_col)
        return pltpu.make_async_remote_copy(
            src_ref=partial.at[s, to_c],
            dst_ref=landed.at[s, c],
            send_sem=p_send.at[k, dc],
            recv_sem=p_recv.at[k, dc],
            device_id=(row, to_c),
            device_id_type=MESH,
        )

    def f_copy(s, k):
        return pltpu.make_async_remote_copy(
            src_ref=final.at[s],
            dst_ref=out_ref.at[c],
            send_sem=f_send.at[k],
            recv_sem=f_recv.at[c],
            device_id=(s * n_lo + l, h),
            device_id_type=MESH,
        )

    def f_near():
        return pltpu.make_async_copy(final.at[h], out_ref.at[c], own_sem.at[2])

    def blocks(d):
        if d == 0:
            return [(0, None, h)]
        return [(2 * d - 1 + side, hears(side, d), h - side_of[side] * d) for side in range(2)]

    def compute(d, q):
        for k, condition, s in blocks(d):
            def run():
                multiply(s, q)
                if q == n_chunk - 1:
                    for dc in range(1, n_col):
                        p_copy(s, k, dc).start()
            run() if condition is None else pl.when(condition)(run)

    def finish(d):
        for k, condition, s in blocks(d):
            def run():
                for dc in range(1, n_col):
                    from_c = lax.rem(c + n_col - dc, n_col)
                    pltpu.make_async_remote_copy(
                        src_ref=landed.at[s, from_c],
                        dst_ref=landed.at[s, from_c],
                        send_sem=p_send.at[k, dc],
                        recv_sem=p_recv.at[k, dc],
                        device_id=(row, c),
                        device_id_type=MESH,
                    ).wait_recv()
                t = rows_at_once(step, 64)

                @pl.loop(0, step // t)
                def _(j):
                    at = pl.ds(0, t) if t == step else pl.ds(pl.multiple_of(j * t, t), t)
                    total = partial[s, c, at, :]
                    for dc in range(1, n_col):
                        total = total + landed[s, lax.rem(c + dc, n_col), at, :]
                    final[s, at, :] = total

                if d == 0:
                    pl.when(c != h)(lambda: f_copy(s, k).start())
                    pl.when(c == h)(lambda: f_near().start())
                else:
                    f_copy(s, k).start()
            run() if condition is None else pl.when(condition)(run)

    chunks = range(n_chunk)
    for q in chunks:
        forward(1, q)
    if n_hi > 2:
        forward(2, 0)
    take_a()
    own_v.wait()
    for q in chunks:
        compute(0, q)
    if n_hi > 2:
        for q in chunks[1:]:
            forward(2, q)
    for d in range(1, n_hi):
        for q in chunks:
            if d > 2:
                forward(d, q)
            compute(d, q)
            if q == 0:
                finish(d - 1)
    finish(n_hi - 1)

    for j in range(n_col):
        @pl.when(jnp.logical_not(is_self(c, j)))
        def _():
            pltpu.make_async_remote_copy(
                src_ref=final.at[0],
                dst_ref=out_ref.at[j],
                send_sem=f_send.at[0],
                recv_sem=f_recv.at[j],
                device_id=(row, c),
                device_id_type=MESH,
            ).wait_recv()
    pl.when(c == h)(lambda: f_near().wait())

    for dl, dc in offsets:
        a_copy(dl, dc).wait_send()
    for side in range(2):
        for d in range(n_hi - 1):
            @pl.when(sends(side, d))
            def _():
                for q in chunks:
                    v_copy(side, d, q).wait_send()
    for d in range(n_hi):
        for k, condition, s in blocks(d):
            def run():
                for dc in range(1, n_col):
                    p_copy(s, k, dc).wait_send()
                if d == 0:
                    pl.when(c != h)(lambda: f_copy(s, k).wait_send())
                else:
                    f_copy(s, k).wait_send()
            run() if condition is None else pl.when(condition)(run)


def per_device(amplitudes, integrals):
    n_row = lax.axis_size("row")
    n_col = lax.axis_size("col")
    n_lo = n_row // n_col
    w, panels, _ = amplitudes.shape
    nb, _, kc = integrals.shape
    rows = w * n_lo * n_col
    kq = tile_of(kc, WIDE)
    n_chunk = kc // kq
    f32, bf16 = jnp.float32, jnp.bfloat16
    dma = pltpu.SemaphoreType.DMA
    step = rows // n_col
    ladder = pl.pallas_call(
        functools.partial(kernel, n_col, n_lo),
        out_shape=jax.ShapeDtypeStruct((n_col, step, nb), f32),
        in_specs=[pl.BlockSpec(memory_space=pl.ANY)] * 2,
        out_specs=pl.BlockSpec(memory_space=pl.ANY),
        scratch_shapes=[
            pltpu.VMEM((rows, panels, kc), f32),
            pltpu.VMEM((n_col, nb, panels, kc), f32),
            pltpu.VMEM((n_col, step, panels * kc), bf16),
            pltpu.VMEM((n_col, step, panels * kc), bf16),
            pltpu.VMEM((nb, panels * kq), bf16),
            pltpu.VMEM((nb, panels * kq), bf16),
            pltpu.VMEM((n_col, n_col, step, nb), f32),
            pltpu.VMEM((n_col, n_col, step, nb), f32),
            pltpu.VMEM((n_col, step, nb), f32),
            dma((3,)),
            dma((n_lo, n_col)),
            dma((n_lo, n_col)),
            dma((2, n_col, n_chunk)),
            dma((2, n_col, n_chunk)),
            dma((2 * n_col, n_col)),
            dma((2 * n_col, n_col)),
            dma((2 * n_col,)),
            dma((n_col,)),
        ],
        compiler_params=pltpu.CompilerParams(
            collective_id=0, has_side_effects=True, vmem_limit_bytes=48 * 2**20
        ),
        cost_estimate=pl.CostEstimate(
            flops=6 * rows * nb * n_col * panels * kc, bytes_accessed=4 * (amplitudes.size + integrals.size), transcendentals=0
        ),
    )(amplitudes, integrals)
    return ladder.reshape(rows, nb)


def solution(mesh):
    in_specs = (P(("row", "col"), None, None), P("row", None, "col"))
    out_specs = P("col", "row")
    return jax.shard_map(
        per_device, mesh=mesh, in_specs=in_specs, out_specs=out_specs, check_vma=False
    )
```
